128 devices in a mesh: blk: 16 (over x, y_hi, core), mate: 8 (over z, y_lo).
Axes of the slice: x: 4, y: 4 (y_hi: 2, y_lo: 2; y = y_hi * 2 + y_lo), z: 4, core: 2. Of those that a mesh axis runs over, the one named last changes fastest.
Arguments:
- record: bfloat16 [128, 1024, 2048], P(('blk', 'mate'))
- starts: int32 [128, 2], P(('blk', 'mate')), may hold values from 0 to 1024, as said below
Outputs:
- correlation: float32 [1024, 1024, 512], P('blk', 'mate')
The draws below stay inside these ranges and needn't reach their ends.
Inputs may be any that keep to these rules, and one draw needn't show every extreme that they name: `starts`: each segment lies inside its window.
All inputs are finite; a program needn't handle non-finite values.
Results may differ from the reference program's by a relative error of at most 0.0059.
Values may be sent and summed in bfloat16 or wider, within the bound.
No kernel may reach another device: no remote copies, remote signals or barrier semaphores. Data moves between devices by JAX's collectives and lax.ppermute only.
A program may use at most 192 MiB of HBM per device.

```python
import math
import jax
import jax.numpy as jnp
from jax import lax

C = 1024
L = 1024
NB = 128
F0 = 4
LAG = 256
WINDOW_LENGTH = 2048
SPW = 2
WINDOW_COUNT = 128
N_BLK = 16


def draw_record(key, part):
    key = jax.random.fold_in(key, 11)
    first, second, third_operand = jax.random.split(key, 3)
    base = jax.random.normal(first, (WINDOW_COUNT, C, WINDOW_LENGTH), jnp.float32)
    upper_limit = math.log(4.0)
    channel = jnp.exp(jax.random.uniform(second, (1, C, 1), jnp.float32) * math.log(10.0))
    transient_events = jnp.exp(jax.random.uniform(third_operand, (WINDOW_COUNT, 1, WINDOW_LENGTH // 64), jnp.float32) * upper_limit)
    amplitude_envelope = jnp.repeat(transient_events, 64, axis=2)
    return (base * channel * amplitude_envelope).astype(jnp.bfloat16)


def draw_starts(key, part):
    key = jax.random.fold_in(key, 23)
    offsets = jax.random.randint(key, (WINDOW_COUNT, SPW), 0, WINDOW_LENGTH - L + 1, dtype=jnp.int32)
    offsets = offsets.at[0, 0].set(0)
    return offsets.at[WINDOW_COUNT - 1, SPW - 1].set(WINDOW_LENGTH - L)


def setup_inputs(seed: int = 0) -> dict:
    streams_of = jax.random.split(jax.random.key(seed), 3)
    record = draw_record(jax.random.fold_in(streams_of[2], 71), 0)
    starts = draw_starts(jax.random.fold_in(streams_of[2], 71), 0)
    return {"record": record, "starts": starts}


def hann_taper(length):
    times = jnp.arange(length, dtype=jnp.int32).astype(jnp.float32)
    return 0.5 - 0.5 * jnp.cos(2.0 * math.pi / length * (times + 0.5))

def frequency_taper(count):
    ramp = max(count // 8, 1)
    index = jnp.arange(count, dtype=jnp.int32).astype(jnp.float32)
    edge = jnp.minimum(jnp.minimum((index + 0.5) / ramp, (count - index - 0.5) / ramp), 1.0)
    return jnp.sin(0.5 * math.pi * edge) ** 2

def dft_table(length):
    times = jnp.arange(length, dtype=jnp.int32)[:, None]
    bins = F0 + jnp.arange(NB, dtype=jnp.int32)[None, :]
    phase = 2.0 * math.pi / length * (times * bins % length).astype(jnp.float32)
    return jnp.concatenate([jnp.cos(phase), -jnp.sin(phase)], 1).astype(jnp.bfloat16)

def lag_table(length):
    bins = F0 + jnp.arange(NB, dtype=jnp.int32)[:, None]
    shifts = jnp.arange(2 * LAG, dtype=jnp.int32)[None, :] - LAG
    phase = 2.0 * math.pi / length * (bins * shifts % length).astype(jnp.float32)
    return jnp.concatenate([jnp.cos(phase), -jnp.sin(phase)], 0).astype(jnp.bfloat16)

def whiten(segs):
    length = segs.shape[-1]
    lead = segs.shape[:-1]
    flat = segs.reshape(-1, length).astype(jnp.float32)
    centred = flat - lax.optimization_barrier(jnp.mean(flat, axis=1, keepdims=True))
    scaled = centred * lax.rsqrt(lax.optimization_barrier(jnp.mean(centred * centred, axis=1, keepdims=True)) + 1e-05)
    tapered = (scaled * hann_taper(length)[None, :]).astype(jnp.bfloat16)
    spectrum = jnp.dot(tapered, dft_table(length), preferred_element_type=jnp.float32)
    count = spectrum.shape[1] // 2
    power = spectrum[:, :count] ** 2 + spectrum[:, count:] ** 2
    level = lax.optimization_barrier(jnp.mean(power, axis=1, keepdims=True))
    gain = frequency_taper(count)[None, :] / jnp.sqrt(power + 0.05 * level + 1e-05)
    whitened = spectrum * jnp.concatenate([gain, gain], 1)
    return whitened.astype(jnp.bfloat16).reshape(lead + (2 * count,))

def pairwise_products(rows, cols, form):
    count = rows.shape[-1] // 2
    real_a, imag_a = (rows[..., :count], rows[..., count:])
    real_b, imag_b = (cols[..., :count], cols[..., count:])
    real = jnp.einsum(form, real_a, real_b) + jnp.einsum(form, imag_a, imag_b)
    imag = jnp.einsum(form, imag_a, real_b) - jnp.einsum(form, real_a, imag_b)
    return jnp.concatenate([real, imag], -1)

def reference(record, starts):

    def one_window(packed):
        window, offsets = packed
        segs = jax.vmap(lambda begin: lax.dynamic_slice_in_dim(window, begin, L, 1))(offsets)
        return whiten(segs)
    spectra = lax.map(one_window, (record, starts))
    block = C // N_BLK
    rows_all = jnp.moveaxis(spectra.reshape(WINDOW_COUNT, SPW, N_BLK, block, 2 * NB), 2, 0)
    every = spectra.astype(jnp.float32)
    table = lag_table(L)
    factor = 1.0 / math.sqrt(WINDOW_COUNT * SPW * NB)

    def one_block(rows):
        cross = pairwise_products(rows.astype(jnp.float32), every, 'wsif,wsjf->ijf')
        rounded = cross.astype(jnp.bfloat16).reshape(-1, 2 * NB)
        lagged = jnp.dot(rounded, table, preferred_element_type=jnp.float32) * factor
        return lagged.reshape(block, C, 2 * LAG)
    result = lax.map(one_block, rows_all)
    return result.reshape(C, C, 2 * LAG)
```

```python
import functools
import math

import jax
import jax.numpy as jnp
import ml_dtypes
import numpy as np
from jax import lax
from jax.experimental import pallas as pl
from jax.experimental.pallas import tpu as pltpu
from jax.sharding import PartitionSpec as P

L = 1024
NB = 128
F0 = 4
LAG = 256
CH = 1024
SEGS = 2
PARTS = 2
LANES = 128
BOTH = ("blk", "mate")

NT = (((1,), (1,)), ((), ()))


def hann_taper(length):
    times = np.arange(length, dtype=np.float64)
    return (0.5 - 0.5 * np.cos(2.0 * math.pi / length * (times + 0.5))).astype(np.float32)


def frequency_taper(count):
    ramp = max(count // 8, 1)
    index = np.arange(count, dtype=np.float64)
    edge = np.minimum(np.minimum((index + 0.5) / ramp, (count - index - 0.5) / ramp), 1.0)
    return (np.sin(0.5 * math.pi * edge) ** 2).astype(np.float32)


def dft_table(length):
    times = np.arange(length)[:, None]
    bins = F0 + np.arange(NB)[None, :]
    phase = 2.0 * math.pi / length * (times * bins % length)
    table = np.concatenate([np.cos(phase), -np.sin(phase)], 1)
    return table.astype(np.float32).astype(ml_dtypes.bfloat16)


def lag_table(length):
    bins = F0 + np.arange(NB)[:, None]
    shifts = np.arange(2 * LAG)[None, :] - LAG
    phase = 2.0 * math.pi / length * (bins * shifts % length)
    table = np.stack([np.cos(phase), -np.sin(phase)], 1).reshape(2 * NB, 2 * LAG)
    return table.astype(np.float32).astype(ml_dtypes.bfloat16)


WCH = 256
WROWS = 32
BLOCKS = CH // LANES
ROWS = BLOCKS * SEGS * PARTS


def whiten_kernel(starts, record, dft, hann, band, out, turned, taper, tapered, held):
    step = pl.program_id(0)

    @pl.when(step == 0)
    def _():
        table = dft[...].astype(jnp.float32)
        for s in range(SEGS):
            shift = lax.rem(starts[0, s], L)
            turned[s] = pltpu.roll(table, shift, 1).astype(jnp.bfloat16)
            taper[s] = pltpu.roll(hann[...], shift, 1)

    late = lax.broadcasted_iota(jnp.int32, (WROWS, L), 1)
    half = lax.rem(step, 2)
    for s in range(SEGS):
        begin = starts[0, s]

        def rows(r, _, s=s, begin=begin):
            at = pl.ds(pl.multiple_of(r * WROWS, WROWS), WROWS)
            first = record[0, at, :L].astype(jnp.float32)
            second = record[0, at, L:].astype(jnp.float32)
            seg = jnp.where(late >= begin, first, second)
            centred = seg - jnp.mean(seg, axis=1, keepdims=True)
            scaled = centred * lax.rsqrt(jnp.mean(centred * centred, axis=1, keepdims=True) + 1e-05)
            tapered[at, :] = (scaled * taper[s, 0:1, :]).astype(jnp.bfloat16)
            return 0

        lax.fori_loop(0, WCH // WROWS, rows, 0, unroll=2)
        spectrum = lax.dot_general(turned[s], tapered[...], NT, preferred_element_type=jnp.float32)
        real, imag = spectrum[:NB], spectrum[NB:]
        power = real * real + imag * imag
        level = jnp.mean(power, axis=0, keepdims=True)
        gain = band[:, 0:1] * lax.rsqrt(power + 0.05 * level + 1e-05)
        for p, part in enumerate((real * gain, imag * gain)):
            for c in range(WCH // LANES):
                row = (half * (WCH // LANES) + c) * SEGS * PARTS + s * PARTS + p
                held[pl.ds(row, NB, stride=ROWS // 2), :] = part[:, c * LANES : (c + 1) * LANES]

    @pl.when(half == 1)
    def _():
        out[...] = held[...].reshape(NB, ROWS // 2, LANES).astype(jnp.bfloat16)


def whiten(record, starts):
    return pl.pallas_call(
        whiten_kernel,
        grid=(CH // WCH,),
        in_specs=[
            pl.BlockSpec(memory_space=pltpu.SMEM),
            pl.BlockSpec((1, WCH, 2 * L), lambda i: (0, i, 0)),
            pl.BlockSpec((2 * NB, L), lambda i: (0, 0)),
            pl.BlockSpec((8, L), lambda i: (0, 0)),
            pl.BlockSpec((NB, LANES), lambda i: (0, 0)),
        ],
        out_specs=pl.BlockSpec((NB, ROWS // 2, LANES), lambda i: (0, i // 2, 0)),
        out_shape=jax.ShapeDtypeStruct((NB, ROWS, LANES), jnp.bfloat16),
        scratch_shapes=[
            pltpu.VMEM((SEGS, 2 * NB, L), jnp.bfloat16),
            pltpu.VMEM((SEGS, 8, L), jnp.float32),
            pltpu.VMEM((WCH, L), jnp.bfloat16),
            pltpu.VMEM((NB * ROWS // 2, LANES), jnp.float32),
        ],
        compiler_params=pltpu.CompilerParams(vmem_limit_bytes=48 * 1024 * 1024),
        name="whiten",
    )(
        starts,
        record,
        jnp.asarray(np.ascontiguousarray(dft_table(L).T)),
        jnp.asarray(np.tile(hann_taper(L)[None], (8, 1))),
        jnp.asarray(np.tile(frequency_taper(NB)[:, None], (1, LANES))),
    )


CROWS = 128


def cross_kernel(windows, spectra, out, wide, left, right):
    step = pl.program_id(0)
    depth = SEGS * windows

    @pl.when(step == 0)
    def _():
        wide[...] = spectra[...].reshape(windows * ROWS, LANES).astype(jnp.float32)
        for c in range(BLOCKS):
            chans = pl.ds(c * LANES, LANES)
            other = pl.ds(CH + c * LANES, LANES)
            for s in range(SEGS):
                for p in range(PARTS):
                    row = c * SEGS * PARTS + s * PARTS + p
                    block = wide[pl.ds(row, windows, stride=ROWS), :]
                    at = pl.ds(p * depth + s * windows, windows)
                    mirror = pl.ds((1 - p) * depth + s * windows, windows)
                    right[at, chans] = block.astype(jnp.bfloat16)
                    right[mirror, other] = (block if p == 0 else -block).astype(jnp.bfloat16)
                    left[chans, at] = block.T.astype(jnp.bfloat16)

    rows = left[pl.ds(pl.multiple_of(step * CROWS, CROWS), CROWS), :]
    for p in range(PARTS):
        product = jnp.dot(rows, right[:, p * CH : (p + 1) * CH], preferred_element_type=jnp.float32)
        product = product.astype(jnp.bfloat16)
        width = out.shape[4]
        for b in range(out.shape[0]):
            for m in range(out.shape[1]):
                out[b, m, p] = product[
                    b * out.shape[3] : (b + 1) * out.shape[3], m * width : (m + 1) * width
                ]


def cross(spectra, blocks, groups):
    windows = spectra.shape[0]
    height, width = CH // blocks, CH // groups
    depth = SEGS * windows
    per = CROWS // height
    return pl.pallas_call(
        functools.partial(cross_kernel, windows),
        grid=(CH // CROWS,),
        in_specs=[pl.BlockSpec((windows, ROWS, LANES), lambda i: (0, 0, 0))],
        out_specs=pl.BlockSpec((per, groups, PARTS, height, width), lambda i: (i, 0, 0, 0, 0)),
        out_shape=jax.ShapeDtypeStruct((blocks, groups, PARTS, height, width), jnp.bfloat16),
        scratch_shapes=[
            pltpu.VMEM((windows * ROWS, LANES), jnp.float32),
            pltpu.VMEM((CH, PARTS * depth), jnp.bfloat16),
            pltpu.VMEM((PARTS * depth, PARTS * CH), jnp.bfloat16),
        ],
        compiler_params=pltpu.CompilerParams(vmem_limit_bytes=48 * 1024 * 1024),
        name="cross",
    )(spectra)


LROWS = 16
LSTEP = 4


def lag_kernel(factor, cross_in, table, out, wide):
    inner = pl.program_id(1)

    @pl.when(inner == 0)
    def _():
        wide[...] = cross_in[...].reshape(wide.shape).astype(jnp.float32)

    for r in range(LSTEP):
        block = wide[pl.ds(inner * LSTEP + r, 2 * NB, stride=LROWS), :]
        lagged = jnp.dot(block.T.astype(jnp.bfloat16), table[...], preferred_element_type=jnp.float32)
        out[r] = lagged * factor


def lag(received, factor):
    bins, height, width = received.shape
    return pl.pallas_call(
        functools.partial(lag_kernel, factor),
        grid=(height // LROWS, LROWS // LSTEP),
        in_specs=[
            pl.BlockSpec((bins, LROWS, width), lambda i, j: (0, i, 0)),
            pl.BlockSpec((bins, 2 * LAG), lambda i, j: (0, 0)),
        ],
        out_specs=pl.BlockSpec(
            (LSTEP, width, 2 * LAG), lambda i, j: (i * (LROWS // LSTEP) + j, 0, 0)
        ),
        out_shape=jax.ShapeDtypeStruct((height, width, 2 * LAG), jnp.float32),
        scratch_shapes=[pltpu.VMEM((bins * LROWS, width), jnp.float32)],
        compiler_params=pltpu.CompilerParams(vmem_limit_bytes=48 * 1024 * 1024),
        name="lag",
    )(received, jnp.asarray(lag_table(L)))


def per_device(record, starts):
    blocks = lax.axis_size("blk")
    groups = lax.axis_size("mate")
    factor = 1.0 / math.sqrt(blocks * groups * SEGS * NB)
    spectra = lax.all_to_all(whiten(record, starts), BOTH, split_axis=0, concat_axis=0, tiled=True)
    pairs = cross(spectra, blocks, groups)
    pairs = pairs.reshape((blocks * groups,) + pairs.shape[2:])
    received = lax.all_to_all(pairs, BOTH, split_axis=0, concat_axis=0, tiled=True)
    received = received.reshape((-1,) + received.shape[2:])
    return lag(received, factor)


def solution(mesh):
    placed = (P(BOTH, None, None), P(BOTH, None))
    return jax.shard_map(
        per_device, mesh=mesh, in_specs=placed, out_specs=P("blk", "mate", None), check_vma=False
    )
```

```python
import functools
import math

import jax
import jax.numpy as jnp
import ml_dtypes
import numpy as np
from jax import lax
from jax.experimental import pallas as pl
from jax.experimental.pallas import tpu as pltpu
from jax.sharding import PartitionSpec as P

L = 1024
NB = 128
F0 = 4
LAG = 256
CH = 1024
SEGS = 2
PARTS = 2
LANES = 128
BOTH = ("blk", "mate")

NT = (((1,), (1,)), ((), ()))


def hann_taper(length):
    times = np.arange(length, dtype=np.float64)
    return (0.5 - 0.5 * np.cos(2.0 * math.pi / length * (times + 0.5))).astype(np.float32)


def frequency_taper(count):
    ramp = max(count // 8, 1)
    index = np.arange(count, dtype=np.float64)
    edge = np.minimum(np.minimum((index + 0.5) / ramp, (count - index - 0.5) / ramp), 1.0)
    return (np.sin(0.5 * math.pi * edge) ** 2).astype(np.float32)


def dft_table(length):
    times = np.arange(length)[:, None]
    bins = F0 + np.arange(NB)[None, :]
    phase = 2.0 * math.pi / length * (times * bins % length)
    table = np.concatenate([np.cos(phase), -np.sin(phase)], 1)
    return table.astype(np.float32).astype(ml_dtypes.bfloat16)


def lag_table(length):
    bins = F0 + np.arange(NB)[:, None]
    shifts = np.arange(2 * LAG)[None, :] - LAG
    phase = 2.0 * math.pi / length * (bins * shifts % length)
    table = np.stack([np.cos(phase), -np.sin(phase)], 1).reshape(2 * NB, 2 * LAG)
    return table.astype(np.float32).astype(ml_dtypes.bfloat16)


WCH = 256
WROWS = 32
BLOCKS = CH // LANES
ROWS = BLOCKS * SEGS * PARTS
ANYWHERE = pl.BlockSpec(memory_space=pltpu.HBM)
RESIDENT = pl.BlockSpec(memory_space=pltpu.VMEM)


def whiten_kernel(
    starts_in, record, dft, hann, band, out, starts, raw, table, window, edge, turned, taper, tapered, held,
    raw_sem, sem,
):
    def fetch(i):
        at = pl.ds(pl.multiple_of(i * WCH, WCH), WCH)
        return pltpu.make_async_copy(record.at[0, at], raw.at[at], raw_sem.at[i])

    small = [
        pltpu.make_async_copy(src, dst, sem.at[i])
        for i, (src, dst) in enumerate(((starts_in, starts), (dft, table), (hann, window), (band, edge)))
    ]
    for copy in small:
        copy.start()
    for i in range(CH // WCH):
        fetch(i).start()
    for copy in small:
        copy.wait()
    for s in range(SEGS):
        shift = lax.rem(starts[0, s], L)
        turned[s] = pltpu.roll(table[...].astype(jnp.float32), shift, 1).astype(jnp.bfloat16)
        taper[s] = pltpu.roll(window[...], shift, 1)
    late = lax.broadcasted_iota(jnp.int32, (WROWS, L), 1)

    def block(i, _):
        fetch(i).wait()
        for s in range(SEGS):
            for r in range(WCH // WROWS):
                at = pl.ds(pl.multiple_of(i * WCH + r * WROWS, WROWS), WROWS)
                first = raw[at, :L].astype(jnp.float32)
                second = raw[at, L:].astype(jnp.float32)
                seg = jnp.where(late >= starts[0, s], first, second)
                centred = seg - jnp.mean(seg, axis=1, keepdims=True)
                scaled = centred * lax.rsqrt(jnp.mean(centred * centred, axis=1, keepdims=True) + 1e-05)
                tapered[s, r * WROWS : (r + 1) * WROWS] = (scaled * taper[s, 0:1, :]).astype(jnp.bfloat16)
        for s in range(SEGS):
            spectrum = lax.dot_general(turned[s], tapered[s], NT, preferred_element_type=jnp.float32)
            real, imag = spectrum[:NB], spectrum[NB:]
            power = real * real + imag * imag
            level = jnp.mean(power, axis=0, keepdims=True)
            gain = edge[:, 0:1] * lax.rsqrt(power + 0.05 * level + 1e-05)
            for p, part in enumerate((real * gain, imag * gain)):
                for c in range(WCH // LANES):
                    row = (i * (WCH // LANES) + c) * SEGS * PARTS + s * PARTS + p
                    held[pl.ds(row, NB, stride=ROWS), :] = part[:, c * LANES : (c + 1) * LANES]
        return 0

    lax.fori_loop(0, CH // WCH, block, 0)
    out[...] = held[...].reshape(NB, ROWS, LANES).astype(jnp.bfloat16)


def whiten(record, starts):
    return pl.pallas_call(
        whiten_kernel,
        in_specs=[ANYWHERE] * 5,
        out_specs=RESIDENT,
        out_shape=jax.ShapeDtypeStruct((NB, ROWS, LANES), jnp.bfloat16),
        scratch_shapes=[
            pltpu.SMEM((1, SEGS), jnp.int32),
            pltpu.VMEM((CH, 2 * L), jnp.bfloat16),
            pltpu.VMEM((2 * NB, L), jnp.bfloat16),
            pltpu.VMEM((8, L), jnp.float32),
            pltpu.VMEM((NB, LANES), jnp.float32),
            pltpu.VMEM((SEGS, 2 * NB, L), jnp.bfloat16),
            pltpu.VMEM((SEGS, 8, L), jnp.float32),
            pltpu.VMEM((SEGS, WCH, L), jnp.bfloat16),
            pltpu.VMEM((NB * ROWS, LANES), jnp.float32),
            pltpu.SemaphoreType.DMA((CH // WCH,)),
            pltpu.SemaphoreType.DMA((4,)),
        ],
        compiler_params=pltpu.CompilerParams(vmem_limit_bytes=48 * 1024 * 1024),
        name="whiten",
    )(
        *(
            pltpu.with_memory_space_constraint(x, pltpu.HBM)
            for x in (
                starts,
                record,
                jnp.asarray(np.ascontiguousarray(dft_table(L).T)),
                jnp.asarray(np.tile(hann_taper(L)[None], (8, 1))),
                jnp.asarray(np.tile(frequency_taper(NB)[:, None], (1, LANES))),
            )
        )
    )


CCOLS = 1024
CPITCH = ROWS + 1


def cross_kernel(windows, spectra, out, wide, left, right):
    depth = SEGS * windows
    blocks, _, _, height, width = out.shape
    for w in range(windows):
        wide[CPITCH * w : CPITCH * w + ROWS] = spectra[w].astype(jnp.float32)
    for c in range(BLOCKS):
        chans = pl.ds(c * LANES, LANES)
        other = pl.ds(CH + c * LANES, LANES)
        for s in range(SEGS):
            for p in range(PARTS):
                row = c * SEGS * PARTS + s * PARTS + p
                block = wide[pl.ds(row, windows, stride=CPITCH), :]
                at = pl.ds(p * depth + s * windows, windows)
                mirror = pl.ds((1 - p) * depth + s * windows, windows)
                right[at, chans] = block.astype(jnp.bfloat16)
                right[mirror, other] = (block if p == 0 else -block).astype(jnp.bfloat16)
                left[chans, at] = block.astype(jnp.bfloat16).T
    for p in range(PARTS):

        def columns(n, _, p=p):
            at = pl.ds(pl.multiple_of(p * CH + n * CCOLS, CCOLS), CCOLS)
            product = jnp.dot(left[...], right[:, at], preferred_element_type=jnp.float32)
            product = product.astype(jnp.bfloat16)
            for b in range(blocks):
                for m in range(CCOLS // width):
                    out[b, n * (CCOLS // width) + m, p] = product[
                        b * height : (b + 1) * height, m * width : (m + 1) * width
                    ]
            return 0

        lax.fori_loop(0, CH // CCOLS, columns, 0)


def cross(spectra, blocks, groups):
    windows = spectra.shape[0]
    height, width = CH // blocks, CH // groups
    depth = SEGS * windows
    return pl.pallas_call(
        functools.partial(cross_kernel, windows),
        in_specs=[RESIDENT],
        out_specs=RESIDENT,
        out_shape=jax.ShapeDtypeStruct((blocks, groups, PARTS, height, width), jnp.bfloat16),
        scratch_shapes=[
            pltpu.VMEM((windows * CPITCH, LANES), jnp.float32),
            pltpu.VMEM((CH, PARTS * depth), jnp.bfloat16),
            pltpu.VMEM((PARTS * depth, PARTS * CH), jnp.bfloat16),
        ],
        compiler_params=pltpu.CompilerParams(vmem_limit_bytes=40 * 1024 * 1024),
        name="cross",
    )(spectra)


LROWS = 16
LPITCH = 17
LSTEP = 4
LSLOTS = 8


def lag_kernel(factor, cross_in, table, out, wide, flat, ready, sem):
    bins, height, width = cross_in.shape
    inner = LROWS // LSTEP
    rounds = height // LROWS

    def put(step):
        slot = lax.rem(step, LSLOTS)
        return pltpu.make_async_copy(ready.at[slot], out.at[pl.ds(step * LSTEP, LSTEP)], sem.at[slot])

    def group(g, _):
        at = pl.ds(pl.multiple_of(g * LROWS, LROWS), LROWS)
        for k in range(bins):
            wide[LPITCH * k : LPITCH * k + LROWS, :] = cross_in[k, at, :].astype(jnp.float32)
        for j in range(inner):
            step = g * inner + j
            for r in range(LSTEP):
                block = wide[pl.ds(j * LSTEP + r, bins, stride=LPITCH), :]
                flat[r * width : (r + 1) * width] = block.astype(jnp.bfloat16).T
            lagged = jnp.dot(flat[...], table[...], preferred_element_type=jnp.float32) * factor

            @pl.when(step >= LSLOTS)
            def _():
                put(step - LSLOTS).wait()

            ready[lax.rem(step, LSLOTS)] = lagged.reshape(LSTEP, width, lagged.shape[-1])
            put(step).start()
        return 0

    lax.fori_loop(0, rounds, group, 0)
    for step in range(max(rounds * inner - LSLOTS, 0), rounds * inner):
        put(step).wait()


def lag(received, factor):
    bins, height, width = received.shape
    return pl.pallas_call(
        functools.partial(lag_kernel, factor),
        in_specs=[RESIDENT, RESIDENT],
        out_specs=ANYWHERE,
        out_shape=jax.ShapeDtypeStruct((height, width, 2 * LAG), jnp.float32),
        scratch_shapes=[
            pltpu.VMEM((bins * LPITCH, width), jnp.float32),
            pltpu.VMEM((LSTEP * width, bins), jnp.bfloat16),
            pltpu.VMEM((LSLOTS, LSTEP, width, 2 * LAG), jnp.float32),
            pltpu.SemaphoreType.DMA((LSLOTS,)),
        ],
        compiler_params=pltpu.CompilerParams(vmem_limit_bytes=40 * 1024 * 1024),
        name="lag",
    )(received, jnp.asarray(lag_table(L)))


def per_device(record, starts):
    blocks = lax.axis_size("blk")
    groups = lax.axis_size("mate")
    factor = 1.0 / math.sqrt(blocks * groups * SEGS * NB)
    spectra = lax.all_to_all(whiten(record, starts), BOTH, split_axis=0, concat_axis=0, tiled=True)
    pairs = cross(spectra, blocks, groups)
    pairs = pairs.reshape((blocks * groups,) + pairs.shape[2:])
    received = lax.all_to_all(pairs, BOTH, split_axis=0, concat_axis=0, tiled=True)
    received = received.reshape((-1,) + received.shape[2:])
    return lag(received, factor)


def solution(mesh):
    placed = (P(BOTH, None, None), P(BOTH, None))
    return jax.shard_map(
        per_device, mesh=mesh, in_specs=placed, out_specs=P("blk", "mate", None), check_vma=False
    )
```

```python
import functools
import math

import jax
import jax.numpy as jnp
import ml_dtypes
import numpy as np
from jax import lax
from jax.experimental import pallas as pl
from jax.experimental.pallas import tpu as pltpu
from jax.sharding import PartitionSpec as P

L = 1024
NB = 128
F0 = 4
LAG = 256
CH = 1024
SEGS = 2
PARTS = 2
LANES = 128
SPLIT = {"x": 4, "yh": 2, "core": 2, "z": 4, "yl": 2}
BLK, MATE = ("x", "yh", "core"), ("z", "yl")
BOTH = BLK + MATE
TURN = ("x", "core", "z", "yl", "yh")

NT = (((1,), (1,)), ((), ()))


def hann_taper(length):
    times = np.arange(length, dtype=np.float64)
    return (0.5 - 0.5 * np.cos(2.0 * math.pi / length * (times + 0.5))).astype(np.float32)


def frequency_taper(count):
    ramp = max(count // 8, 1)
    index = np.arange(count, dtype=np.float64)
    edge = np.minimum(np.minimum((index + 0.5) / ramp, (count - index - 0.5) / ramp), 1.0)
    return (np.sin(0.5 * math.pi * edge) ** 2).astype(np.float32)


def dft_table(length):
    times = np.arange(length)[:, None]
    bins = F0 + np.arange(NB)[None, :]
    phase = 2.0 * math.pi / length * (times * bins % length)
    table = np.concatenate([np.cos(phase), -np.sin(phase)], 1)
    return table.astype(np.float32).astype(ml_dtypes.bfloat16)


def lag_table(length):
    bins = F0 + np.arange(NB)[:, None]
    shifts = np.arange(2 * LAG)[None, :] - LAG
    phase = 2.0 * math.pi / length * (bins * shifts % length)
    table = np.stack([np.cos(phase), -np.sin(phase)], 1).reshape(2 * NB, 2 * LAG)
    return table.astype(np.float32).astype(ml_dtypes.bfloat16)


WCH = 256
WROWS = 32
BLOCKS = CH // LANES
ROWS = BLOCKS * SEGS * PARTS
HPITCH = ROWS + 1
ANYWHERE = pl.BlockSpec(memory_space=pltpu.HBM)
RESIDENT = pl.BlockSpec(memory_space=pltpu.VMEM)


def whiten_kernel(
    starts_in, record, dft, hann, band, out, starts, raw, table, window, edge, turned, taper, chosen, tapered,
    held, raw_sem, sem,
):

    def fetch(i):
        at = pl.ds(pl.multiple_of(i * WCH, WCH), WCH)
        return pltpu.make_async_copy(record.at[0, at], raw.at[at], raw_sem.at[i])

    small = [
        pltpu.make_async_copy(src, dst, sem.at[i])
        for i, (src, dst) in enumerate(((starts_in, starts), (dft, table), (hann, window), (band, edge)))
    ]
    fetch(0).start()
    for copy in small:
        copy.start()
    fetch(1).start()
    for copy in small:
        copy.wait()
    for s in range(SEGS):
        shift = lax.rem(starts[0, s], L)
        turned[s] = pltpu.roll(table[...].astype(jnp.float32), shift, 1).astype(jnp.bfloat16)
        taper[s] = pltpu.roll(window[...], shift, 1)

    def prepare(i, s):
        passed = lax.broadcasted_iota(jnp.int32, (WROWS, L), 1) >= starts[0, s]
        sums, squares = [], []
        for r in range(WCH // WROWS):
            at = pl.ds(pl.multiple_of(i * WCH + r * WROWS, WROWS), WROWS)
            seg = jnp.where(passed, raw[at, :L], raw[at, L:])
            chosen[s, r * WROWS : (r + 1) * WROWS] = seg
            sums.append(jnp.sum(seg.astype(jnp.float32), axis=1, keepdims=True))
        means = [jnp.broadcast_to(x * (1.0 / L), (WROWS, LANES)) for x in sums]
        for r in range(WCH // WROWS):
            seg = chosen[s, r * WROWS : (r + 1) * WROWS].astype(jnp.float32)
            total = None
            for t in range(L // LANES):
                centred = seg[:, t * LANES : (t + 1) * LANES] - means[r]
                total = centred * centred if total is None else total + centred * centred
            squares.append(jnp.sum(total, axis=1, keepdims=True))
        scales = [jnp.broadcast_to(lax.rsqrt(x * (1.0 / L) + 1e-05), (WROWS, LANES)) for x in squares]
        for r in range(WCH // WROWS):
            seg = chosen[s, r * WROWS : (r + 1) * WROWS].astype(jnp.float32)
            for t in range(L // LANES):
                at = slice(t * LANES, (t + 1) * LANES)
                scaled = (seg[:, at] - means[r]) * scales[r]
                tapered[s, pl.ds(pl.multiple_of(i * WCH + r * WROWS, WROWS), WROWS), at] = (scaled * taper[s, 0:1, at]).astype(jnp.bfloat16)

    def transform(s):
        spectrum = lax.dot_general(turned[s], tapered[s], NT, preferred_element_type=jnp.float32)
        for c in range(BLOCKS):
            real, imag = (spectrum[p * NB : (p + 1) * NB, c * LANES : (c + 1) * LANES] for p in range(PARTS))
            power = real * real + imag * imag
            level = jnp.mean(power, axis=0, keepdims=True)
            gain = edge[...] * lax.rsqrt(power + 0.05 * level + 1e-05)
            for p, part in enumerate((real * gain, imag * gain)):
                held[pl.ds(c * SEGS * PARTS + s * PARTS + p, NB, stride=HPITCH), :] = part

    count = CH // WCH

    def block(i, _):
        fetch(i).wait()

        @pl.when(i + 2 < count)
        def _():
            fetch(i + 2).start()

        for s in range(SEGS):
            prepare(i, s)
        return 0

    lax.fori_loop(0, count, block, 0)
    for s in range(SEGS):
        transform(s)
    for k in range(NB):
        out[k] = held[HPITCH * k : HPITCH * k + ROWS].astype(jnp.bfloat16)


def whiten(record, starts):
    return pl.pallas_call(
        whiten_kernel,
        in_specs=[ANYWHERE] * 5,
        out_specs=RESIDENT,
        out_shape=jax.ShapeDtypeStruct((NB, ROWS, LANES), jnp.bfloat16),
        scratch_shapes=[
            pltpu.SMEM((1, SEGS), jnp.int32),
            pltpu.VMEM((CH, 2 * L), jnp.bfloat16),
            pltpu.VMEM((2 * NB, L), jnp.bfloat16),
            pltpu.VMEM((8, L), jnp.float32),
            pltpu.VMEM((NB, LANES), jnp.float32),
            pltpu.VMEM((SEGS, 2 * NB, L), jnp.bfloat16),
            pltpu.VMEM((SEGS, 8, L), jnp.float32),
            pltpu.VMEM((SEGS, WCH, L), jnp.bfloat16),
            pltpu.VMEM((SEGS, CH, L), jnp.bfloat16),
            pltpu.VMEM((NB * HPITCH, LANES), jnp.float32),
            pltpu.SemaphoreType.DMA((CH // WCH,)),
            pltpu.SemaphoreType.DMA((4,)),
        ],
        compiler_params=pltpu.CompilerParams(vmem_limit_bytes=48 * 1024 * 1024),
        name="whiten",
    )(
        *(
            pltpu.with_memory_space_constraint(x, pltpu.HBM)
            for x in (
                starts,
                record,
                jnp.asarray(np.ascontiguousarray(dft_table(L).T)),
                jnp.asarray(np.tile(hann_taper(L)[None], (8, 1))),
                jnp.asarray(np.tile(frequency_taper(NB)[:, None], (1, LANES))),
            )
        )
    )


CPITCH = ROWS + 1


def cross_kernel(windows, spectra, out, wide, left, right):
    depth = SEGS * windows
    height, width = out.shape[-2:]
    for w in range(windows):
        wide[CPITCH * w : CPITCH * w + ROWS] = spectra[w].astype(jnp.float32)
    for c in range(BLOCKS):
        chans = pl.ds(c * LANES, LANES)
        other = pl.ds(CH + c * LANES, LANES)
        for s in range(SEGS):
            for p in range(PARTS):
                row = c * SEGS * PARTS + s * PARTS + p
                block = wide[pl.ds(row, windows, stride=CPITCH), :]
                at = pl.ds(p * depth + s * windows, windows)
                mirror = pl.ds((1 - p) * depth + s * windows, windows)
                right[at, chans] = block.astype(jnp.bfloat16)
                right[mirror, other] = (block if p == 0 else -block).astype(jnp.bfloat16)
                left[chans, at] = block.astype(jnp.bfloat16).T
    for p in range(PARTS):
        product = jnp.dot(left[...], right[:, p * CH : (p + 1) * CH], preferred_element_type=jnp.float32)
        product = product.astype(jnp.bfloat16)
        for b in range(CH // height):
            for m in range(CH // width):
                place = dict(zip(SPLIT, np.unravel_index(b * (CH // width) + m, tuple(SPLIT.values()))))
                out[tuple(int(place[a]) for a in TURN) + (p,)] = product[
                    b * height : (b + 1) * height, m * width : (m + 1) * width
                ]


def cross(spectra, blocks, groups):
    windows = spectra.shape[0]
    height, width = CH // blocks, CH // groups
    depth = SEGS * windows
    return pl.pallas_call(
        functools.partial(cross_kernel, windows),
        in_specs=[RESIDENT],
        out_specs=RESIDENT,
        out_shape=jax.ShapeDtypeStruct(
            tuple(SPLIT[a] for a in TURN) + (PARTS, height, width), jnp.bfloat16
        ),
        scratch_shapes=[
            pltpu.VMEM((windows * CPITCH, LANES), jnp.float32),
            pltpu.VMEM((CH, PARTS * depth), jnp.bfloat16),
            pltpu.VMEM((PARTS * depth, PARTS * CH), jnp.bfloat16),
        ],
        compiler_params=pltpu.CompilerParams(vmem_limit_bytes=40 * 1024 * 1024),
        name="cross",
    )(spectra)


LROWS = 16
LPITCH = 17
LSTEP = 8
LSLOTS = 4


def lag_kernel(factor, cross_in, table, out, wide, flat, ready, sem):
    bins, height, width = cross_in.shape
    inner = LROWS // LSTEP
    rounds = height // LROWS

    def put(step):
        slot = lax.rem(step, LSLOTS)
        return pltpu.make_async_copy(ready.at[slot], out.at[pl.ds(step * LSTEP, LSTEP)], sem.at[slot])

    def group(g, _):
        at = pl.ds(pl.multiple_of(g * LROWS, LROWS), LROWS)
        for k in range(bins):
            wide[LPITCH * k : LPITCH * k + LROWS, :] = cross_in[k, at, :].astype(jnp.float32)
        for j in range(inner):
            step = g * inner + j
            for r in range(LSTEP):
                block = wide[pl.ds(j * LSTEP + r, bins, stride=LPITCH), :]
                flat[r * width : (r + 1) * width] = block.astype(jnp.bfloat16).T
            lagged = jnp.dot(flat[...], table[...], preferred_element_type=jnp.float32) * factor

            @pl.when(step >= LSLOTS)
            def _():
                put(step - LSLOTS).wait()

            ready[lax.rem(step, LSLOTS)] = lagged.reshape(LSTEP, width, lagged.shape[-1])
            put(step).start()
        return 0

    lax.fori_loop(0, rounds, group, 0)
    for step in range(max(rounds * inner - LSLOTS, 0), rounds * inner):
        put(step).wait()


def lag(received, factor):
    bins, height, width = received.shape
    return pl.pallas_call(
        functools.partial(lag_kernel, factor),
        in_specs=[RESIDENT, RESIDENT],
        out_specs=ANYWHERE,
        out_shape=jax.ShapeDtypeStruct((height, width, 2 * LAG), jnp.float32),
        scratch_shapes=[
            pltpu.VMEM((bins * LPITCH, width), jnp.float32),
            pltpu.VMEM((LSTEP * width, bins), jnp.bfloat16),
            pltpu.VMEM((LSLOTS, LSTEP, width, 2 * LAG), jnp.float32),
            pltpu.SemaphoreType.DMA((LSLOTS,)),
        ],
        compiler_params=pltpu.CompilerParams(vmem_limit_bytes=40 * 1024 * 1024),
        name="lag",
    )(received, jnp.asarray(lag_table(L)))


def exchange(x):
    return lax.all_to_all(x, TURN, split_axis=0, concat_axis=0, tiled=True)


def per_device(record, starts):
    blocks = lax.axis_size(BLK)
    groups = lax.axis_size(MATE)
    factor = 1.0 / math.sqrt(blocks * groups * SEGS * NB)
    spectra = exchange(whiten(record, starts))
    pairs = cross(spectra, blocks, groups)
    received = exchange(pairs.reshape((blocks * groups,) + pairs.shape[-3:]))
    return lag(received.reshape((-1,) + received.shape[2:]), factor)


def solution(mesh):
    fine = jax.sharding.Mesh(mesh.devices.reshape(tuple(SPLIT.values())), tuple(SPLIT))
    placed = (P(BOTH, None, None), P(BOTH, None))
    return jax.shard_map(
        per_device, mesh=fine, in_specs=placed, out_specs=P(BLK, MATE, None), check_vma=False
    )
```

```python
import functools
import math

import jax
import jax.numpy as jnp
import ml_dtypes
import numpy as np
from jax import lax
from jax.experimental import pallas as pl
from jax.experimental.pallas import tpu as pltpu
from jax.sharding import PartitionSpec as P

L = 1024
NB = 128
F0 = 4
LAG = 256
CH = 1024
SEGS = 2
PARTS = 2
LANES = 128
SPLIT = {"x": 4, "yh": 2, "core": 2, "z": 4, "yl": 2}
BLK, MATE = ("x", "yh", "core"), ("z", "yl")
BOTH = BLK + MATE
TURN = ("x", "core", "z", "yl", "yh")

NT = (((1,), (1,)), ((), ()))


def hann_taper(length):
    times = np.arange(length, dtype=np.float64)
    return (0.5 - 0.5 * np.cos(2.0 * math.pi / length * (times + 0.5))).astype(np.float32)


def frequency_taper(count):
    ramp = max(count // 8, 1)
    index = np.arange(count, dtype=np.float64)
    edge = np.minimum(np.minimum((index + 0.5) / ramp, (count - index - 0.5) / ramp), 1.0)
    return (np.sin(0.5 * math.pi * edge) ** 2).astype(np.float32)


def dft_table(length):
    times = np.arange(length)[:, None]
    bins = F0 + np.arange(NB)[None, :]
    phase = 2.0 * math.pi / length * (times * bins % length)
    table = np.concatenate([np.cos(phase), -np.sin(phase)], 1)
    return table.astype(np.float32).astype(ml_dtypes.bfloat16)


def lag_table(length):
    bins = F0 + np.arange(NB)[:, None]
    shifts = np.arange(2 * LAG)[None, :] - LAG
    phase = 2.0 * math.pi / length * (bins * shifts % length)
    table = np.stack([np.cos(phase), -np.sin(phase)], 1).reshape(2 * NB, 2 * LAG)
    return table.astype(np.float32).astype(ml_dtypes.bfloat16)


WCH = 256
WROWS = 32
BLOCKS = CH // LANES
ROWS = BLOCKS * SEGS * PARTS
HPITCH = ROWS + 1
ANYWHERE = pl.BlockSpec(memory_space=pltpu.HBM)
RESIDENT = pl.BlockSpec(memory_space=pltpu.VMEM)


def whiten_kernel(
    starts_in, record, dft, hann, band, out, starts, raw, table, window, edge, turned, taper, chosen, tapered,
    held, raw_sem, sem,
):

    def fetch(i):
        at = pl.ds(i * WCH, WCH)
        return pltpu.make_async_copy(record.at[0, at], raw.at[at], raw_sem.at[i])

    small = [
        pltpu.make_async_copy(src, dst, sem.at[i])
        for i, (src, dst) in enumerate(((starts_in, starts), (dft, table), (hann, window), (band, edge)))
    ]
    fetch(0).start()
    for copy in small:
        copy.start()
    fetch(1).start()
    for copy in small:
        copy.wait()
    for s in range(SEGS):
        shift = lax.rem(starts[0, s], L)
        taper[s] = pltpu.roll(window[...], shift, 1)

    def prepare(i, s):
        passed = lax.broadcasted_iota(jnp.int32, (WROWS, L), 1) >= starts[0, s]
        sums, squares = [], []
        for r in range(WCH // WROWS):
            at = pl.ds(i * WCH + r * WROWS, WROWS)
            seg = jnp.where(passed, raw[at, :L], raw[at, L:])
            chosen[s, r * WROWS : (r + 1) * WROWS] = seg
            sums.append(jnp.sum(seg.astype(jnp.float32), axis=1, keepdims=True))
        means = [jnp.broadcast_to(x * (1.0 / L), (WROWS, LANES)) for x in sums]
        for r in range(WCH // WROWS):
            seg = chosen[s, r * WROWS : (r + 1) * WROWS].astype(jnp.float32)
            total = None
            for t in range(L // LANES):
                centred = seg[:, t * LANES : (t + 1) * LANES] - means[r]
                total = centred * centred if total is None else total + centred * centred
            squares.append(jnp.sum(total, axis=1, keepdims=True))
        scales = [jnp.broadcast_to(lax.rsqrt(x * (1.0 / L) + 1e-05), (WROWS, LANES)) for x in squares]
        for r in range(WCH // WROWS):
            seg = chosen[s, r * WROWS : (r + 1) * WROWS].astype(jnp.float32)
            for t in range(L // LANES):
                at = slice(t * LANES, (t + 1) * LANES)
                scaled = (seg[:, at] - means[r]) * scales[r]
                tapered[s, pl.ds(i * WCH + r * WROWS, WROWS), at] = (scaled * taper[s, 0:1, at]).astype(jnp.bfloat16)

    def transform(s):
        shift = lax.rem(starts[0, s], L)
        turned[s] = pltpu.roll(table[...].astype(jnp.float32), shift, 1).astype(jnp.bfloat16)
        spectrum = lax.dot_general(turned[s], tapered[s], NT, preferred_element_type=jnp.float32)
        for c in range(BLOCKS):
            real, imag = (spectrum[p * NB : (p + 1) * NB, c * LANES : (c + 1) * LANES] for p in range(PARTS))
            power = real * real + imag * imag
            level = jnp.mean(power, axis=0, keepdims=True)
            gain = edge[...] * lax.rsqrt(power + 0.05 * level + 1e-05)
            for p, part in enumerate((real * gain, imag * gain)):
                held[pl.ds(c * SEGS * PARTS + s * PARTS + p, NB, stride=HPITCH), :] = part

    count = CH // WCH

    for i in range(count):
        fetch(i).wait()
        if i + 2 < count:
            fetch(i + 2).start()
        for s in range(SEGS):
            prepare(i, s)
    for s in range(SEGS):
        transform(s)
    for k in range(NB):
        out[k] = held[HPITCH * k : HPITCH * k + ROWS].astype(jnp.bfloat16)


def whiten(record, starts):
    return pl.pallas_call(
        whiten_kernel,
        in_specs=[ANYWHERE] * 5,
        out_specs=RESIDENT,
        out_shape=jax.ShapeDtypeStruct((NB, ROWS, LANES), jnp.bfloat16),
        scratch_shapes=[
            pltpu.SMEM((1, SEGS), jnp.int32),
            pltpu.VMEM((CH, 2 * L), jnp.bfloat16),
            pltpu.VMEM((2 * NB, L), jnp.bfloat16),
            pltpu.VMEM((8, L), jnp.float32),
            pltpu.VMEM((NB, LANES), jnp.float32),
            pltpu.VMEM((SEGS, 2 * NB, L), jnp.bfloat16),
            pltpu.VMEM((SEGS, 8, L), jnp.float32),
            pltpu.VMEM((SEGS, WCH, L), jnp.bfloat16),
            pltpu.VMEM((SEGS, CH, L), jnp.bfloat16),
            pltpu.VMEM((NB * HPITCH, LANES), jnp.float32),
            pltpu.SemaphoreType.DMA((CH // WCH,)),
            pltpu.SemaphoreType.DMA((4,)),
        ],
        compiler_params=pltpu.CompilerParams(vmem_limit_bytes=48 * 1024 * 1024),
        name="whiten",
    )(
        *(
            pltpu.with_memory_space_constraint(x, pltpu.HBM)
            for x in (
                starts,
                record,
                jnp.asarray(np.ascontiguousarray(dft_table(L).T)),
                jnp.asarray(np.tile(hann_taper(L)[None], (8, 1))),
                jnp.asarray(np.tile(frequency_taper(NB)[:, None], (1, LANES))),
            )
        )
    )


CPITCH = ROWS + 1


def cross_kernel(windows, spectra, out, wide, left, right):
    depth = SEGS * windows
    height, width = out.shape[-2:]
    for w in range(windows):
        wide[CPITCH * w : CPITCH * w + ROWS] = spectra[w].astype(jnp.float32)
    for c in range(BLOCKS):
        chans = pl.ds(c * LANES, LANES)
        other = pl.ds(CH + c * LANES, LANES)
        for s in range(SEGS):
            for p in range(PARTS):
                row = c * SEGS * PARTS + s * PARTS + p
                block = wide[pl.ds(row, windows, stride=CPITCH), :]
                at = pl.ds(p * depth + s * windows, windows)
                mirror = pl.ds((1 - p) * depth + s * windows, windows)
                right[at, chans] = block.astype(jnp.bfloat16)
                right[mirror, other] = (block if p == 0 else -block).astype(jnp.bfloat16)
                left[chans, at] = block.astype(jnp.bfloat16).T
    for p in range(PARTS):
        product = jnp.dot(left[...], right[:, p * CH : (p + 1) * CH], preferred_element_type=jnp.float32)
        product = product.astype(jnp.bfloat16)
        for b in range(CH // height):
            for m in range(CH // width):
                place = dict(zip(SPLIT, np.unravel_index(b * (CH // width) + m, tuple(SPLIT.values()))))
                out[tuple(int(place[a]) for a in TURN) + (p,)] = product[
                    b * height : (b + 1) * height, m * width : (m + 1) * width
                ]


def cross(spectra, blocks, groups):
    windows = spectra.shape[0]
    height, width = CH // blocks, CH // groups
    depth = SEGS * windows
    return pl.pallas_call(
        functools.partial(cross_kernel, windows),
        in_specs=[RESIDENT],
        out_specs=RESIDENT,
        out_shape=jax.ShapeDtypeStruct(
            tuple(SPLIT[a] for a in TURN) + (PARTS, height, width), jnp.bfloat16
        ),
        scratch_shapes=[
            pltpu.VMEM((windows * CPITCH, LANES), jnp.float32),
            pltpu.VMEM((CH, PARTS * depth), jnp.bfloat16),
            pltpu.VMEM((PARTS * depth, PARTS * CH), jnp.bfloat16),
        ],
        compiler_params=pltpu.CompilerParams(vmem_limit_bytes=40 * 1024 * 1024),
        name="cross",
    )(spectra)


LROWS = 16
LPITCH = 17
LSTEP = 16
LSLOTS = 3


def lag_kernel(factor, cross_in, table, out, wide, flat, ready, sem):
    bins, height, width = cross_in.shape
    inner = LROWS // LSTEP
    rounds = height // LROWS

    def put(step):
        slot = lax.rem(step, LSLOTS)
        return pltpu.make_async_copy(ready.at[slot], out.at[pl.ds(step * LSTEP, LSTEP)], sem.at[slot])

    def group(g, _):
        at = pl.ds(pl.multiple_of(g * LROWS, LROWS), LROWS)
        for k in range(bins):
            wide[LPITCH * k : LPITCH * k + LROWS, :] = cross_in[k, at, :].astype(jnp.float32)
        for j in range(inner):
            step = g * inner + j
            for r in range(LSTEP):
                block = wide[pl.ds(j * LSTEP + r, bins, stride=LPITCH), :]
                flat[r * width : (r + 1) * width] = block.astype(jnp.bfloat16).T
            lagged = jnp.dot(flat[...], table[...], preferred_element_type=jnp.float32) * factor

            @pl.when(step >= LSLOTS)
            def _():
                put(step - LSLOTS).wait()

            ready[lax.rem(step, LSLOTS)] = lagged.reshape(LSTEP, width, lagged.shape[-1])
            put(step).start()
        return 0

    lax.fori_loop(0, rounds, group, 0)
    for step in range(max(rounds * inner - LSLOTS, 0), rounds * inner):
        put(step).wait()


def lag(received, factor):
    bins, height, width = received.shape
    return pl.pallas_call(
        functools.partial(lag_kernel, factor),
        in_specs=[RESIDENT, RESIDENT],
        out_specs=ANYWHERE,
        out_shape=jax.ShapeDtypeStruct((height, width, 2 * LAG), jnp.float32),
        scratch_shapes=[
            pltpu.VMEM((bins * LPITCH, width), jnp.float32),
            pltpu.VMEM((LSTEP * width, bins), jnp.bfloat16),
            pltpu.VMEM((LSLOTS, LSTEP, width, 2 * LAG), jnp.float32),
            pltpu.SemaphoreType.DMA((LSLOTS,)),
        ],
        compiler_params=pltpu.CompilerParams(vmem_limit_bytes=40 * 1024 * 1024),
        name="lag",
    )(received, jnp.asarray(lag_table(L)))


def exchange(x):
    return lax.all_to_all(x, TURN, split_axis=0, concat_axis=0, tiled=True)


def per_device(record, starts):
    blocks = lax.axis_size(BLK)
    groups = lax.axis_size(MATE)
    factor = 1.0 / math.sqrt(blocks * groups * SEGS * NB)
    spectra = exchange(whiten(record, starts))
    pairs = cross(spectra, blocks, groups)
    received = exchange(pairs.reshape((blocks * groups,) + pairs.shape[-3:]))
    return lag(received.reshape((-1,) + received.shape[2:]), factor)


def solution(mesh):
    fine = jax.sharding.Mesh(mesh.devices.reshape(tuple(SPLIT.values())), tuple(SPLIT))
    placed = (P(BOTH, None, None), P(BOTH, None))
    return jax.shard_map(
        per_device, mesh=fine, in_specs=placed, out_specs=P(BLK, MATE, None), check_vma=False
    )
```

```python
import functools
import math

import jax
import jax.numpy as jnp
import ml_dtypes
import numpy as np
from jax import lax
from jax.experimental import pallas as pl
from jax.experimental.pallas import tpu as pltpu
from jax.sharding import PartitionSpec as P

L = 1024
NB = 128
F0 = 4
LAG = 256
CH = 1024
SEGS = 2
PARTS = 2
LANES = 128
SPLIT = {"x": 4, "yh": 2, "core": 2, "z": 4, "yl": 2}
BLK, MATE = ("x", "yh", "core"), ("z", "yl")
BOTH = BLK + MATE
TURN = ("yh", "yl", "core", "z", "x")

NT = (((1,), (1,)), ((), ()))


def hann_taper(length):
    times = np.arange(length, dtype=np.float64)
    return (0.5 - 0.5 * np.cos(2.0 * math.pi / length * (times + 0.5))).astype(np.float32)


def frequency_taper(count):
    ramp = max(count // 8, 1)
    index = np.arange(count, dtype=np.float64)
    edge = np.minimum(np.minimum((index + 0.5) / ramp, (count - index - 0.5) / ramp), 1.0)
    return (np.sin(0.5 * math.pi * edge) ** 2).astype(np.float32)


def dft_table(length):
    times = np.arange(length)[:, None]
    bins = F0 + np.arange(NB)[None, :]
    phase = 2.0 * math.pi / length * (times * bins % length)
    table = np.concatenate([np.cos(phase), -np.sin(phase)], 1)
    return table.astype(np.float32).astype(ml_dtypes.bfloat16)


def lag_table(length):
    bins = F0 + np.arange(NB)[:, None]
    shifts = np.arange(2 * LAG)[None, :] - LAG
    phase = 2.0 * math.pi / length * (bins * shifts % length)
    table = np.stack([np.cos(phase), -np.sin(phase)], 1).reshape(2 * NB, 2 * LAG)
    return table.astype(np.float32).astype(ml_dtypes.bfloat16)


WCH = 256
WROWS = 32
BLOCKS = CH // LANES
ROWS = BLOCKS * SEGS * PARTS
HPITCH = ROWS + 1
ANYWHERE = pl.BlockSpec(memory_space=pltpu.HBM)
RESIDENT = pl.BlockSpec(memory_space=pltpu.VMEM)


def whiten_kernel(
    starts_in, record, dft, hann, band, out, starts, raw, table, window, edge, turned, taper, chosen, tapered,
    held, raw_sem, sem,
):

    def fetch(i):
        at = pl.ds(i * WCH, WCH)
        return pltpu.make_async_copy(record.at[0, at], raw.at[at], raw_sem.at[i])

    small = [
        pltpu.make_async_copy(src, dst, sem.at[i])
        for i, (src, dst) in enumerate(((starts_in, starts), (dft, table), (hann, window), (band, edge)))
    ]
    fetch(0).start()
    for copy in small:
        copy.start()
    fetch(1).start()
    for copy in small:
        copy.wait()
    for s in range(SEGS):
        shift = lax.rem(starts[0, s], L)
        taper[s] = pltpu.roll(window[...], shift, 1)

    def prepare(i, s):
        passed = lax.broadcasted_iota(jnp.int32, (WROWS, L), 1) >= starts[0, s]
        sums, squares = [], []
        for r in range(WCH // WROWS):
            at = pl.ds(i * WCH + r * WROWS, WROWS)
            seg = jnp.where(passed, raw[at, :L], raw[at, L:])
            chosen[s, r * WROWS : (r + 1) * WROWS] = seg
            sums.append(jnp.sum(seg.astype(jnp.float32), axis=1, keepdims=True))
        means = [jnp.broadcast_to(x * (1.0 / L), (WROWS, LANES)) for x in sums]
        for r in range(WCH // WROWS):
            seg = chosen[s, r * WROWS : (r + 1) * WROWS].astype(jnp.float32)
            total = None
            for t in range(L // LANES):
                centred = seg[:, t * LANES : (t + 1) * LANES] - means[r]
                total = centred * centred if total is None else total + centred * centred
            squares.append(jnp.sum(total, axis=1, keepdims=True))
        scales = [jnp.broadcast_to(lax.rsqrt(x * (1.0 / L) + 1e-05), (WROWS, LANES)) for x in squares]
        for r in range(WCH // WROWS):
            seg = chosen[s, r * WROWS : (r + 1) * WROWS].astype(jnp.float32)
            for t in range(L // LANES):
                at = slice(t * LANES, (t + 1) * LANES)
                scaled = (seg[:, at] - means[r]) * scales[r]
                tapered[s, pl.ds(i * WCH + r * WROWS, WROWS), at] = (scaled * taper[s, 0:1, at]).astype(jnp.bfloat16)

    def transform(s):
        shift = lax.rem(starts[0, s], L)
        turned[s] = pltpu.roll(table[...].astype(jnp.float32), shift, 1).astype(jnp.bfloat16)
        spectrum = lax.dot_general(turned[s], tapered[s], NT, preferred_element_type=jnp.float32)
        for c in range(BLOCKS):
            real, imag = (spectrum[p * NB : (p + 1) * NB, c * LANES : (c + 1) * LANES] for p in range(PARTS))
            power = real * real + imag * imag
            level = jnp.mean(power, axis=0, keepdims=True)
            gain = edge[...] * lax.rsqrt(power + 0.05 * level + 1e-05)
            for p, part in enumerate((real * gain, imag * gain)):
                held[pl.ds(c * SEGS * PARTS + s * PARTS + p, NB, stride=HPITCH), :] = part

    count = CH // WCH

    for i in range(count):
        fetch(i).wait()
        if i + 2 < count:
            fetch(i + 2).start()
        for s in range(SEGS):
            prepare(i, s)
    for s in range(SEGS):
        transform(s)
    for k in range(NB):
        out[k] = held[HPITCH * k : HPITCH * k + ROWS].astype(jnp.bfloat16)


def whiten(record, starts):
    return pl.pallas_call(
        whiten_kernel,
        in_specs=[ANYWHERE] * 5,
        out_specs=RESIDENT,
        out_shape=jax.ShapeDtypeStruct((NB, ROWS, LANES), jnp.bfloat16),
        scratch_shapes=[
            pltpu.SMEM((1, SEGS), jnp.int32),
            pltpu.VMEM((CH, 2 * L), jnp.bfloat16),
            pltpu.VMEM((2 * NB, L), jnp.bfloat16),
            pltpu.VMEM((8, L), jnp.float32),
            pltpu.VMEM((NB, LANES), jnp.float32),
            pltpu.VMEM((SEGS, 2 * NB, L), jnp.bfloat16),
            pltpu.VMEM((SEGS, 8, L), jnp.float32),
            pltpu.VMEM((SEGS, WCH, L), jnp.bfloat16),
            pltpu.VMEM((SEGS, CH, L), jnp.bfloat16),
            pltpu.VMEM((NB * HPITCH, LANES), jnp.float32),
            pltpu.SemaphoreType.DMA((CH // WCH,)),
            pltpu.SemaphoreType.DMA((4,)),
        ],
        compiler_params=pltpu.CompilerParams(vmem_limit_bytes=48 * 1024 * 1024),
        name="whiten",
    )(
        *(
            pltpu.with_memory_space_constraint(x, pltpu.HBM)
            for x in (
                starts,
                record,
                jnp.asarray(np.ascontiguousarray(dft_table(L).T)),
                jnp.asarray(np.tile(hann_taper(L)[None], (8, 1))),
                jnp.asarray(np.tile(frequency_taper(NB)[:, None], (1, LANES))),
            )
        )
    )


CPITCH = ROWS + 1


def cross_kernel(windows, spectra, out, wide, left, right):
    depth = SEGS * windows
    height, width = out.shape[-2:]
    for w in range(windows):
        wide[CPITCH * w : CPITCH * w + ROWS] = spectra[w].astype(jnp.float32)
    for c in range(BLOCKS):
        chans = pl.ds(c * LANES, LANES)
        other = pl.ds(CH + c * LANES, LANES)
        for s in range(SEGS):
            for p in range(PARTS):
                row = c * SEGS * PARTS + s * PARTS + p
                block = wide[pl.ds(row, windows, stride=CPITCH), :]
                at = pl.ds(p * depth + s * windows, windows)
                mirror = pl.ds((1 - p) * depth + s * windows, windows)
                right[at, chans] = block.astype(jnp.bfloat16)
                right[mirror, other] = (block if p == 0 else -block).astype(jnp.bfloat16)
                left[chans, at] = block.astype(jnp.bfloat16).T
    for p in range(PARTS):
        product = jnp.dot(left[...], right[:, p * CH : (p + 1) * CH], preferred_element_type=jnp.float32)
        product = product.astype(jnp.bfloat16)
        for b in range(CH // height):
            for m in range(CH // width):
                place = dict(zip(SPLIT, np.unravel_index(b * (CH // width) + m, tuple(SPLIT.values()))))
                out[tuple(int(place[a]) for a in TURN) + (p,)] = product[
                    b * height : (b + 1) * height, m * width : (m + 1) * width
                ]


def cross(spectra, blocks, groups):
    windows = spectra.shape[0]
    height, width = CH // blocks, CH // groups
    depth = SEGS * windows
    return pl.pallas_call(
        functools.partial(cross_kernel, windows),
        in_specs=[RESIDENT],
        out_specs=RESIDENT,
        out_shape=jax.ShapeDtypeStruct(
            tuple(SPLIT[a] for a in TURN) + (PARTS, height, width), jnp.bfloat16
        ),
        scratch_shapes=[
            pltpu.VMEM((windows * CPITCH, LANES), jnp.float32),
            pltpu.VMEM((CH, PARTS * depth), jnp.bfloat16),
            pltpu.VMEM((PARTS * depth, PARTS * CH), jnp.bfloat16),
        ],
        compiler_params=pltpu.CompilerParams(vmem_limit_bytes=40 * 1024 * 1024),
        name="cross",
    )(spectra)


LROWS = 16
LPITCH = 17
LSTEP = 16
LSLOTS = 3


def lag_kernel(factor, cross_in, table, out, wide, flat, ready, sem):
    bins, height, width = cross_in.shape
    inner = LROWS // LSTEP
    rounds = height // LROWS

    def put(step):
        slot = lax.rem(step, LSLOTS)
        return pltpu.make_async_copy(ready.at[slot], out.at[pl.ds(step * LSTEP, LSTEP)], sem.at[slot])

    def group(g, _):
        at = pl.ds(pl.multiple_of(g * LROWS, LROWS), LROWS)
        for k in range(bins):
            wide[LPITCH * k : LPITCH * k + LROWS, :] = cross_in[k, at, :].astype(jnp.float32)
        for j in range(inner):
            step = g * inner + j
            for r in range(LSTEP):
                block = wide[pl.ds(j * LSTEP + r, bins, stride=LPITCH), :]
                flat[r * width : (r + 1) * width] = block.astype(jnp.bfloat16).T
            lagged = jnp.dot(flat[...], table[...], preferred_element_type=jnp.float32) * factor

            @pl.when(step >= LSLOTS)
            def _():
                put(step - LSLOTS).wait()

            ready[lax.rem(step, LSLOTS)] = lagged.reshape(LSTEP, width, lagged.shape[-1])
            put(step).start()
        return 0

    lax.fori_loop(0, rounds, group, 0)
    for step in range(max(rounds * inner - LSLOTS, 0), rounds * inner):
        put(step).wait()


def lag(received, factor):
    bins, height, width = received.shape
    return pl.pallas_call(
        functools.partial(lag_kernel, factor),
        in_specs=[RESIDENT, RESIDENT],
        out_specs=ANYWHERE,
        out_shape=jax.ShapeDtypeStruct((height, width, 2 * LAG), jnp.float32),
        scratch_shapes=[
            pltpu.VMEM((bins * LPITCH, width), jnp.float32),
            pltpu.VMEM((LSTEP * width, bins), jnp.bfloat16),
            pltpu.VMEM((LSLOTS, LSTEP, width, 2 * LAG), jnp.float32),
            pltpu.SemaphoreType.DMA((LSLOTS,)),
        ],
        compiler_params=pltpu.CompilerParams(vmem_limit_bytes=40 * 1024 * 1024),
        name="lag",
    )(received, jnp.asarray(lag_table(L)))


def exchange(x):
    return lax.all_to_all(x, TURN, split_axis=0, concat_axis=0, tiled=True)


def per_device(record, starts):
    blocks = lax.axis_size(BLK)
    groups = lax.axis_size(MATE)
    factor = 1.0 / math.sqrt(blocks * groups * SEGS * NB)
    spectra = exchange(whiten(record, starts))
    pairs = cross(spectra, blocks, groups)
    received = exchange(pairs.reshape((blocks * groups,) + pairs.shape[-3:]))
    return lag(received.reshape((-1,) + received.shape[2:]), factor)


def solution(mesh):
    fine = jax.sharding.Mesh(mesh.devices.reshape(tuple(SPLIT.values())), tuple(SPLIT))
    placed = (P(BOTH, None, None), P(BOTH, None))
    return jax.shard_map(
        per_device, mesh=fine, in_specs=placed, out_specs=P(BLK, MATE, None), check_vma=False
    )
```

```python
import functools
import math

import jax
import jax.numpy as jnp
import ml_dtypes
import numpy as np
from jax import lax
from jax.experimental import pallas as pl
from jax.experimental.pallas import tpu as pltpu
from jax.sharding import PartitionSpec as P

L = 1024
NB = 128
F0 = 4
LAG = 256
CH = 1024
SEGS = 2
PARTS = 2
LANES = 128
SPARE = 64
SPLIT = {"x": 4, "yh": 2, "core": 2, "z": 4, "yl": 2}
BLK, MATE = ("x", "yh", "core"), ("z", "yl")
BOTH = BLK + MATE
TURN = ("yh", "yl", "core", "z", "x")

NT = (((1,), (1,)), ((), ()))


def hann_taper(length):
    times = np.arange(length, dtype=np.float64)
    return (0.5 - 0.5 * np.cos(2.0 * math.pi / length * (times + 0.5))).astype(np.float32)


def frequency_taper(count):
    ramp = max(count // 8, 1)
    index = np.arange(count, dtype=np.float64)
    edge = np.minimum(np.minimum((index + 0.5) / ramp, (count - index - 0.5) / ramp), 1.0)
    return (np.sin(0.5 * math.pi * edge) ** 2).astype(np.float32)


def dft_table(length):
    times = np.arange(length)[:, None]
    bins = F0 + np.arange(NB)[None, :]
    phase = 2.0 * math.pi / length * (times * bins % length)
    table = np.concatenate([np.cos(phase), -np.sin(phase)], 1)
    return table.astype(np.float32).astype(ml_dtypes.bfloat16)


def lag_table(length):
    bins = F0 + np.arange(NB)[:, None]
    shifts = np.arange(2 * LAG)[None, :] - LAG
    phase = 2.0 * math.pi / length * (bins * shifts % length)
    table = np.stack([np.cos(phase), -np.sin(phase)], 1).reshape(2 * NB, 2 * LAG)
    return table.astype(np.float32).astype(ml_dtypes.bfloat16)


WCH = 256
WROWS = 32
BLOCKS = CH // LANES
ROWS = BLOCKS * SEGS * PARTS
HPITCH = ROWS + 1
ANYWHERE = pl.BlockSpec(memory_space=pltpu.HBM)
RESIDENT = pl.BlockSpec(memory_space=pltpu.VMEM)


def whiten_kernel(
    starts_in, record, dft, hann, band, out, starts, raw, table, window, edge, turned, taper, chosen, tapered,
    held, raw_sem, sem,
):

    def fetch(i):
        at = pl.ds(i * WCH, WCH)
        return pltpu.make_async_copy(record.at[0, at], raw.at[at], raw_sem.at[i])

    small = [
        pltpu.make_async_copy(src, dst, sem.at[i])
        for i, (src, dst) in enumerate(((starts_in, starts), (dft, table), (hann, window), (band, edge)))
    ]
    fetch(0).start()
    for copy in small:
        copy.start()
    fetch(1).start()
    for copy in small:
        copy.wait()
    for s in range(SEGS):
        shift = lax.rem(starts[0, s], L)
        taper[s] = pltpu.roll(window[...], shift, 1)

    def prepare(i, s):
        passed = lax.broadcasted_iota(jnp.int32, (WROWS, L), 1) >= starts[0, s]
        sums, squares = [], []
        for r in range(WCH // WROWS):
            at = pl.ds(i * WCH + r * WROWS, WROWS)
            seg = jnp.where(passed, raw[at, :L], raw[at, L:])
            chosen[s, r * WROWS : (r + 1) * WROWS] = seg
            sums.append(jnp.sum(seg.astype(jnp.float32), axis=1, keepdims=True))
        means = [jnp.broadcast_to(x * (1.0 / L), (WROWS, LANES)) for x in sums]
        for r in range(WCH // WROWS):
            seg = chosen[s, r * WROWS : (r + 1) * WROWS].astype(jnp.float32)
            total = None
            for t in range(L // LANES):
                centred = seg[:, t * LANES : (t + 1) * LANES] - means[r]
                total = centred * centred if total is None else total + centred * centred
            squares.append(jnp.sum(total, axis=1, keepdims=True))
        scales = [jnp.broadcast_to(lax.rsqrt(x * (1.0 / L) + 1e-05), (WROWS, LANES)) for x in squares]
        for r in range(WCH // WROWS):
            seg = chosen[s, r * WROWS : (r + 1) * WROWS].astype(jnp.float32)
            for t in range(L // LANES):
                at = slice(t * LANES, (t + 1) * LANES)
                scaled = (seg[:, at] - means[r]) * scales[r]
                tapered[s, pl.ds(i * WCH + r * WROWS, WROWS), at] = (scaled * taper[s, 0:1, at]).astype(jnp.bfloat16)

    def transform(s):
        shift = lax.rem(starts[0, s], L)
        turned[s] = pltpu.roll(table[...].astype(jnp.float32), shift, 1).astype(jnp.bfloat16)
        spectrum = lax.dot_general(turned[s], tapered[s], NT, preferred_element_type=jnp.float32)
        for c in range(BLOCKS):
            real, imag = (spectrum[p * NB : (p + 1) * NB, c * LANES : (c + 1) * LANES] for p in range(PARTS))
            power = real * real + imag * imag
            level = jnp.mean(power, axis=0, keepdims=True)
            gain = edge[...] * lax.rsqrt(power + 0.05 * level + 1e-05)
            for p, part in enumerate((real * gain, imag * gain)):
                held[pl.ds(c * SEGS * PARTS + s * PARTS + p, NB, stride=HPITCH), :] = part

    count = CH // WCH

    for i in range(count):
        fetch(i).wait()
        if i + 2 < count:
            fetch(i + 2).start()
        for s in range(SEGS):
            prepare(i, s)
    for s in range(SEGS):
        transform(s)
    for k in range(NB):
        out[k] = held[HPITCH * k : HPITCH * k + ROWS].astype(jnp.bfloat16)


def whiten(record, starts):
    return pl.pallas_call(
        whiten_kernel,
        in_specs=[ANYWHERE] * 5,
        out_specs=RESIDENT,
        out_shape=jax.ShapeDtypeStruct((NB, ROWS, LANES), jnp.bfloat16),
        scratch_shapes=[
            pltpu.SMEM((1, SEGS), jnp.int32),
            pltpu.VMEM((CH, 2 * L), jnp.bfloat16),
            pltpu.VMEM((2 * NB, L), jnp.bfloat16),
            pltpu.VMEM((8, L), jnp.float32),
            pltpu.VMEM((NB, LANES), jnp.float32),
            pltpu.VMEM((SEGS, 2 * NB, L), jnp.bfloat16),
            pltpu.VMEM((SEGS, 8, L), jnp.float32),
            pltpu.VMEM((SEGS, WCH, L), jnp.bfloat16),
            pltpu.VMEM((SEGS, CH, L), jnp.bfloat16),
            pltpu.VMEM((NB * HPITCH + SPARE, LANES), jnp.float32),
            pltpu.SemaphoreType.DMA((CH // WCH,)),
            pltpu.SemaphoreType.DMA((4,)),
        ],
        compiler_params=pltpu.CompilerParams(vmem_limit_bytes=48 * 1024 * 1024),
        name="whiten",
    )(
        *(
            pltpu.with_memory_space_constraint(x, pltpu.HBM)
            for x in (
                starts,
                record,
                jnp.asarray(np.ascontiguousarray(dft_table(L).T)),
                jnp.asarray(np.tile(hann_taper(L)[None], (8, 1))),
                jnp.asarray(np.tile(frequency_taper(NB)[:, None], (1, LANES))),
            )
        )
    )


CPITCH = ROWS + 1


def cross_kernel(windows, spectra, out, wide, left, right):
    depth = SEGS * windows
    height, width = out.shape[-2:]
    for w in range(windows):
        wide[CPITCH * w : CPITCH * w + ROWS] = spectra[w].astype(jnp.float32)
    for c in range(BLOCKS):
        chans = pl.ds(c * LANES, LANES)
        other = pl.ds(CH + c * LANES, LANES)
        for s in range(SEGS):
            for p in range(PARTS):
                row = c * SEGS * PARTS + s * PARTS + p
                block = wide[pl.ds(row, windows, stride=CPITCH), :]
                at = pl.ds(p * depth + s * windows, windows)
                mirror = pl.ds((1 - p) * depth + s * windows, windows)
                right[at, chans] = block.astype(jnp.bfloat16)
                right[mirror, other] = (block if p == 0 else -block).astype(jnp.bfloat16)
                left[chans, at] = block.astype(jnp.bfloat16).T
    for p in range(PARTS):
        product = jnp.dot(left[...], right[:, p * CH : (p + 1) * CH], preferred_element_type=jnp.float32)
        product = product.astype(jnp.bfloat16)
        for b in range(CH // height):
            for m in range(CH // width):
                place = dict(zip(SPLIT, np.unravel_index(b * (CH // width) + m, tuple(SPLIT.values()))))
                out[tuple(int(place[a]) for a in TURN) + (p,)] = product[
                    b * height : (b + 1) * height, m * width : (m + 1) * width
                ]


def cross(spectra, blocks, groups):
    windows = spectra.shape[0]
    height, width = CH // blocks, CH // groups
    depth = SEGS * windows
    return pl.pallas_call(
        functools.partial(cross_kernel, windows),
        in_specs=[RESIDENT],
        out_specs=RESIDENT,
        out_shape=jax.ShapeDtypeStruct(
            tuple(SPLIT[a] for a in TURN) + (PARTS, height, width), jnp.bfloat16
        ),
        scratch_shapes=[
            pltpu.VMEM((windows * CPITCH + SPARE, LANES), jnp.float32),
            pltpu.VMEM((CH, PARTS * depth), jnp.bfloat16),
            pltpu.VMEM((PARTS * depth, PARTS * CH), jnp.bfloat16),
        ],
        compiler_params=pltpu.CompilerParams(vmem_limit_bytes=40 * 1024 * 1024),
        name="cross",
    )(spectra)


LROWS = 16
LPITCH = 17
LSTEP = 16
LSLOTS = 3


def lag_kernel(factor, cross_in, table, out, wide, flat, ready, sem):
    bins, height, width = cross_in.shape
    inner = LROWS // LSTEP
    rounds = height // LROWS

    def put(step):
        slot = lax.rem(step, LSLOTS)
        return pltpu.make_async_copy(ready.at[slot], out.at[pl.ds(step * LSTEP, LSTEP)], sem.at[slot])

    def group(g, _):
        at = pl.ds(pl.multiple_of(g * LROWS, LROWS), LROWS)
        for k in range(bins):
            wide[LPITCH * k : LPITCH * k + LROWS, :] = cross_in[k, at, :].astype(jnp.float32)
        for j in range(inner):
            step = g * inner + j
            for r in range(LSTEP):
                block = wide[pl.ds(j * LSTEP + r, bins, stride=LPITCH), :]
                flat[r * width : (r + 1) * width] = block.astype(jnp.bfloat16).T
            lagged = jnp.dot(flat[...], table[...], preferred_element_type=jnp.float32) * factor

            @pl.when(step >= LSLOTS)
            def _():
                put(step - LSLOTS).wait()

            ready[lax.rem(step, LSLOTS)] = lagged.reshape(LSTEP, width, lagged.shape[-1])
            put(step).start()
        return 0

    lax.fori_loop(0, rounds, group, 0)
    for step in range(max(rounds * inner - LSLOTS, 0), rounds * inner):
        put(step).wait()


def lag(received, factor):
    bins, height, width = received.shape
    return pl.pallas_call(
        functools.partial(lag_kernel, factor),
        in_specs=[RESIDENT, RESIDENT],
        out_specs=ANYWHERE,
        out_shape=jax.ShapeDtypeStruct((height, width, 2 * LAG), jnp.float32),
        scratch_shapes=[
            pltpu.VMEM((bins * LPITCH + SPARE, width), jnp.float32),
            pltpu.VMEM((LSTEP * width, bins), jnp.bfloat16),
            pltpu.VMEM((LSLOTS, LSTEP, width, 2 * LAG), jnp.float32),
            pltpu.SemaphoreType.DMA((LSLOTS,)),
        ],
        compiler_params=pltpu.CompilerParams(vmem_limit_bytes=40 * 1024 * 1024),
        name="lag",
    )(received, jnp.asarray(lag_table(L)))


def exchange(x):
    return lax.all_to_all(x, TURN, split_axis=0, concat_axis=0, tiled=True)


def per_device(record, starts):
    blocks = lax.axis_size(BLK)
    groups = lax.axis_size(MATE)
    factor = 1.0 / math.sqrt(blocks * groups * SEGS * NB)
    spectra = exchange(whiten(record, starts))
    pairs = cross(spectra, blocks, groups)
    received = exchange(pairs.reshape((blocks * groups,) + pairs.shape[-3:]))
    return lag(received.reshape((-1,) + received.shape[2:]), factor)


def solution(mesh):
    fine = jax.sharding.Mesh(mesh.devices.reshape(tuple(SPLIT.values())), tuple(SPLIT))
    placed = (P(BOTH, None, None), P(BOTH, None))
    return jax.shard_map(
        per_device, mesh=fine, in_specs=placed, out_specs=P(BLK, MATE, None), check_vma=False
    )
```

```python
import functools
import math

import jax
import jax.numpy as jnp
import ml_dtypes
import numpy as np
from jax import lax
from jax.experimental import pallas as pl
from jax.experimental.pallas import tpu as pltpu
from jax.sharding import PartitionSpec as P

L = 1024
NB = 128
F0 = 4
LAG = 256
CH = 1024
SEGS = 2
PARTS = 2
LANES = 128
SPARE = 64
SPLIT = {"x": 4, "yh": 2, "core": 2, "z": 4, "yl": 2}
BLK, MATE = ("x", "yh", "core"), ("z", "yl")
BOTH = BLK + MATE
TURN = ("yh", "yl", "core", "z", "x")
FIRST = ("yl", "z", "core", "yh", "x")

NT = (((1,), (1,)), ((), ()))


def hann_taper(length):
    times = np.arange(length, dtype=np.float64)
    return (0.5 - 0.5 * np.cos(2.0 * math.pi / length * (times + 0.5))).astype(np.float32)


def frequency_taper(count):
    ramp = max(count // 8, 1)
    index = np.arange(count, dtype=np.float64)
    edge = np.minimum(np.minimum((index + 0.5) / ramp, (count - index - 0.5) / ramp), 1.0)
    return (np.sin(0.5 * math.pi * edge) ** 2).astype(np.float32)


def dft_table(length):
    times = np.arange(length)[:, None]
    bins = F0 + np.arange(NB)[None, :]
    phase = 2.0 * math.pi / length * (times * bins % length)
    table = np.concatenate([np.cos(phase), -np.sin(phase)], 1)
    return table.astype(np.float32).astype(ml_dtypes.bfloat16)


def lag_table(length):
    bins = F0 + np.arange(NB)[:, None]
    shifts = np.arange(2 * LAG)[None, :] - LAG
    phase = 2.0 * math.pi / length * (bins * shifts % length)
    table = np.stack([np.cos(phase), -np.sin(phase)], 1).reshape(2 * NB, 2 * LAG)
    return table.astype(np.float32).astype(ml_dtypes.bfloat16)


WCH = 256
WROWS = 32
BLOCKS = CH // LANES
ROWS = BLOCKS * SEGS * PARTS
HPITCH = ROWS + 1
ANYWHERE = pl.BlockSpec(memory_space=pltpu.HBM)
RESIDENT = pl.BlockSpec(memory_space=pltpu.VMEM)


def whiten_kernel(
    starts_in, record, dft, hann, band, out, starts, raw, table, window, edge, turned, taper, chosen, tapered,
    held, raw_sem, sem,
):

    def fetch(i):
        at = pl.ds(i * WCH, WCH)
        return pltpu.make_async_copy(record.at[0, at], raw.at[at], raw_sem.at[i])

    small = [
        pltpu.make_async_copy(src, dst, sem.at[i])
        for i, (src, dst) in enumerate(((starts_in, starts), (dft, table), (hann, window), (band, edge)))
    ]
    fetch(0).start()
    for copy in small:
        copy.start()
    fetch(1).start()
    for copy in small:
        copy.wait()
    for s in range(SEGS):
        shift = lax.rem(starts[0, s], L)
        taper[s] = pltpu.roll(window[...], shift, 1)

    def prepare(i, s):
        passed = lax.broadcasted_iota(jnp.int32, (WROWS, L), 1) >= starts[0, s]
        sums, squares = [], []
        for r in range(WCH // WROWS):
            at = pl.ds(i * WCH + r * WROWS, WROWS)
            seg = jnp.where(passed, raw[at, :L], raw[at, L:])
            chosen[s, r * WROWS : (r + 1) * WROWS] = seg
            sums.append(jnp.sum(seg.astype(jnp.float32), axis=1, keepdims=True))
        means = [jnp.broadcast_to(x * (1.0 / L), (WROWS, LANES)) for x in sums]
        for r in range(WCH // WROWS):
            seg = chosen[s, r * WROWS : (r + 1) * WROWS].astype(jnp.float32)
            total = None
            for t in range(L // LANES):
                centred = seg[:, t * LANES : (t + 1) * LANES] - means[r]
                total = centred * centred if total is None else total + centred * centred
            squares.append(jnp.sum(total, axis=1, keepdims=True))
        scales = [jnp.broadcast_to(lax.rsqrt(x * (1.0 / L) + 1e-05), (WROWS, LANES)) for x in squares]
        for r in range(WCH // WROWS):
            seg = chosen[s, r * WROWS : (r + 1) * WROWS].astype(jnp.float32)
            for t in range(L // LANES):
                at = slice(t * LANES, (t + 1) * LANES)
                scaled = (seg[:, at] - means[r]) * scales[r]
                tapered[s, pl.ds(i * WCH + r * WROWS, WROWS), at] = (scaled * taper[s, 0:1, at]).astype(jnp.bfloat16)

    def transform(s):
        shift = lax.rem(starts[0, s], L)
        turned[s] = pltpu.roll(table[...].astype(jnp.float32), shift, 1).astype(jnp.bfloat16)
        spectrum = lax.dot_general(turned[s], tapered[s], NT, preferred_element_type=jnp.float32)
        for c in range(BLOCKS):
            real, imag = (spectrum[p * NB : (p + 1) * NB, c * LANES : (c + 1) * LANES] for p in range(PARTS))
            power = real * real + imag * imag
            level = jnp.mean(power, axis=0, keepdims=True)
            gain = edge[...] * lax.rsqrt(power + 0.05 * level + 1e-05)
            for p, part in enumerate((real * gain, imag * gain)):
                held[pl.ds(c * SEGS * PARTS + s * PARTS + p, NB, stride=HPITCH), :] = part

    count = CH // WCH

    for i in range(count):
        fetch(i).wait()
        if i + 2 < count:
            fetch(i + 2).start()
        for s in range(SEGS):
            prepare(i, s)
    for s in range(SEGS):
        transform(s)
    for k in range(NB):
        place = dict(zip(FIRST, np.unravel_index(k, tuple(SPLIT[a] for a in FIRST))))
        row = HPITCH * int(np.ravel_multi_index([place[a] for a in TURN], [SPLIT[a] for a in TURN]))
        out[k] = held[row : row + ROWS].astype(jnp.bfloat16)


def whiten(record, starts):
    return pl.pallas_call(
        whiten_kernel,
        in_specs=[ANYWHERE] * 5,
        out_specs=RESIDENT,
        out_shape=jax.ShapeDtypeStruct((NB, ROWS, LANES), jnp.bfloat16),
        scratch_shapes=[
            pltpu.SMEM((1, SEGS), jnp.int32),
            pltpu.VMEM((CH, 2 * L), jnp.bfloat16),
            pltpu.VMEM((2 * NB, L), jnp.bfloat16),
            pltpu.VMEM((8, L), jnp.float32),
            pltpu.VMEM((NB, LANES), jnp.float32),
            pltpu.VMEM((SEGS, 2 * NB, L), jnp.bfloat16),
            pltpu.VMEM((SEGS, 8, L), jnp.float32),
            pltpu.VMEM((SEGS, WCH, L), jnp.bfloat16),
            pltpu.VMEM((SEGS, CH, L), jnp.bfloat16),
            pltpu.VMEM((NB * HPITCH + SPARE, LANES), jnp.float32),
            pltpu.SemaphoreType.DMA((CH // WCH,)),
            pltpu.SemaphoreType.DMA((4,)),
        ],
        compiler_params=pltpu.CompilerParams(vmem_limit_bytes=48 * 1024 * 1024),
        name="whiten",
    )(
        *(
            pltpu.with_memory_space_constraint(x, pltpu.HBM)
            for x in (
                starts,
                record,
                jnp.asarray(np.ascontiguousarray(dft_table(L).T)),
                jnp.asarray(np.tile(hann_taper(L)[None], (8, 1))),
                jnp.asarray(np.tile(frequency_taper(NB)[:, None], (1, LANES))),
            )
        )
    )


CPITCH = ROWS + 1


def cross_kernel(windows, spectra, out, wide, left, right):
    depth = SEGS * windows
    height, width = out.shape[-2:]
    for w in range(windows):
        wide[CPITCH * w : CPITCH * w + ROWS] = spectra[w].astype(jnp.float32)
    for c in range(BLOCKS):
        chans = pl.ds(c * LANES, LANES)
        other = pl.ds(CH + c * LANES, LANES)
        for s in range(SEGS):
            for p in range(PARTS):
                row = c * SEGS * PARTS + s * PARTS + p
                block = wide[pl.ds(row, windows, stride=CPITCH), :]
                at = pl.ds(p * depth + s * windows, windows)
                mirror = pl.ds((1 - p) * depth + s * windows, windows)
                right[at, chans] = block.astype(jnp.bfloat16)
                right[mirror, other] = (block if p == 0 else -block).astype(jnp.bfloat16)
                left[chans, at] = block.astype(jnp.bfloat16).T
    for p in range(PARTS):
        product = jnp.dot(left[...], right[:, p * CH : (p + 1) * CH], preferred_element_type=jnp.float32)
        product = product.astype(jnp.bfloat16)
        for b in range(CH // height):
            for m in range(CH // width):
                place = dict(zip(SPLIT, np.unravel_index(b * (CH // width) + m, tuple(SPLIT.values()))))
                out[tuple(int(place[a]) for a in TURN) + (p,)] = product[
                    b * height : (b + 1) * height, m * width : (m + 1) * width
                ]


def cross(spectra, blocks, groups):
    windows = spectra.shape[0]
    height, width = CH // blocks, CH // groups
    depth = SEGS * windows
    return pl.pallas_call(
        functools.partial(cross_kernel, windows),
        in_specs=[RESIDENT],
        out_specs=RESIDENT,
        out_shape=jax.ShapeDtypeStruct(
            tuple(SPLIT[a] for a in TURN) + (PARTS, height, width), jnp.bfloat16
        ),
        scratch_shapes=[
            pltpu.VMEM((windows * CPITCH + SPARE, LANES), jnp.float32),
            pltpu.VMEM((CH, PARTS * depth), jnp.bfloat16),
            pltpu.VMEM((PARTS * depth, PARTS * CH), jnp.bfloat16),
        ],
        compiler_params=pltpu.CompilerParams(vmem_limit_bytes=40 * 1024 * 1024),
        name="cross",
    )(spectra)


LROWS = 16
LPITCH = 17
LSTEP = 16
LSLOTS = 3


def lag_kernel(factor, cross_in, table, out, wide, flat, ready, sem):
    bins, height, width = cross_in.shape
    inner = LROWS // LSTEP
    rounds = height // LROWS

    def put(step):
        slot = lax.rem(step, LSLOTS)
        return pltpu.make_async_copy(ready.at[slot], out.at[pl.ds(step * LSTEP, LSTEP)], sem.at[slot])

    def group(g, _):
        at = pl.ds(pl.multiple_of(g * LROWS, LROWS), LROWS)
        for k in range(bins):
            wide[LPITCH * k : LPITCH * k + LROWS, :] = cross_in[k, at, :].astype(jnp.float32)
        for j in range(inner):
            step = g * inner + j
            for r in range(LSTEP):
                block = wide[pl.ds(j * LSTEP + r, bins, stride=LPITCH), :]
                flat[r * width : (r + 1) * width] = block.astype(jnp.bfloat16).T
            lagged = jnp.dot(flat[...], table[...], preferred_element_type=jnp.float32) * factor

            @pl.when(step >= LSLOTS)
            def _():
                put(step - LSLOTS).wait()

            ready[lax.rem(step, LSLOTS)] = lagged.reshape(LSTEP, width, lagged.shape[-1])
            put(step).start()
        return 0

    lax.fori_loop(0, rounds, group, 0)
    for step in range(max(rounds * inner - LSLOTS, 0), rounds * inner):
        put(step).wait()


def lag(received, factor):
    bins, height, width = received.shape
    return pl.pallas_call(
        functools.partial(lag_kernel, factor),
        in_specs=[RESIDENT, RESIDENT],
        out_specs=ANYWHERE,
        out_shape=jax.ShapeDtypeStruct((height, width, 2 * LAG), jnp.float32),
        scratch_shapes=[
            pltpu.VMEM((bins * LPITCH + SPARE, width), jnp.float32),
            pltpu.VMEM((LSTEP * width, bins), jnp.bfloat16),
            pltpu.VMEM((LSLOTS, LSTEP, width, 2 * LAG), jnp.float32),
            pltpu.SemaphoreType.DMA((LSLOTS,)),
        ],
        compiler_params=pltpu.CompilerParams(vmem_limit_bytes=40 * 1024 * 1024),
        name="lag",
    )(received, jnp.asarray(lag_table(L)))


def exchange(x, order):
    return lax.all_to_all(x, order, split_axis=0, concat_axis=0, tiled=True)


def per_device(record, starts):
    blocks = lax.axis_size(BLK)
    groups = lax.axis_size(MATE)
    factor = 1.0 / math.sqrt(blocks * groups * SEGS * NB)
    spectra = exchange(whiten(record, starts), FIRST)
    pairs = cross(spectra, blocks, groups)
    received = exchange(pairs.reshape((blocks * groups,) + pairs.shape[-3:]), TURN)
    return lag(received.reshape((-1,) + received.shape[2:]), factor)


def solution(mesh):
    fine = jax.sharding.Mesh(mesh.devices.reshape(tuple(SPLIT.values())), tuple(SPLIT))
    placed = (P(BOTH, None, None), P(BOTH, None))
    return jax.shard_map(
        per_device, mesh=fine, in_specs=placed, out_specs=P(BLK, MATE, None), check_vma=False
    )
```
